32 devices in a mesh: lon: 8 (over z, core), lat: 4 (over y, x).
Axes of the slice: x: 2, y: 2, z: 4, core: 2. Of those that a mesh axis runs over, the one named last changes fastest.
Arguments:
- tracers: float32 [4, 512, 256, 128], P(None, 'lon', 'lat'), may hold values from 0.2 to 2
- kdiff: float32 [512, 256, 128], P('lon', 'lat'), may hold values from 0.3 to 8
- photolysis: float32 [512, 256, 128], P('lon', 'lat'), may hold values from 0.05 to 2
- u_wind: float32 [512, 256, 128], P('lon', 'lat'), may hold values from -0.24 to 0.24
- v_wind: float32 [512, 256, 128], P('lon', 'lat'), may hold values from -0.24 to 0.24
- day_count: int32 [8, 4], replicated, may hold values from 0 to 32, as said below
- day_order: int32 [8, 4, 32], P('lon', 'lat'), may hold values from 0 to 31, each once within a row
Outputs:
- tracers_next: float32 [4, 512, 256, 128], P(None, 'lon', 'lat')
The draws below stay inside these ranges and needn't reach their ends.
Inputs may be any that keep to these rules, and one draw needn't show every extreme that they name: Tile (i, j) has day_count[i, j] daylit blocks, named by the first entries of day_order[i, j, :].
All inputs are finite; a program needn't handle non-finite values.
Results may differ from the reference program's by a relative error of at most 0.00002.
Values sent between devices are 32-bit elements; how exact they have to be, the bound alone decides.
No kernel may reach another device: no remote copies, remote signals or barrier semaphores. Data moves between devices by JAX's collectives and lax.ppermute only.
A program may use at most 128 MiB of HBM per device.

```python
import math
import jax
import jax.numpy as jnp
from jax import lax

CLON = 64
CLAT = 64
LEV = 128
SPECIES = 4
BCOL = 128
SECTIONS = 12
TLON = 8
TLAT = 4
NLON = 512
NLAT = 256
BLK = 32
HALF = 16


def draw_day_count(key, part):
    key_phase = jax.random.fold_in(key, 11)
    key_lit = jax.random.fold_in(key, 23)
    key_dark = jax.random.fold_in(key, 37)
    phase = jax.random.randint(key_phase, (), 0, TLON)
    lon_tiles = jnp.arange(TLON, dtype=jnp.int32)[:, None]
    lat_tiles = jnp.arange(TLAT, dtype=jnp.int32)[None, :]
    row_phase = phase + lat_tiles % 2 * (TLON // 2)
    relative = (lon_tiles - row_phase) % TLON
    dayside = relative < TLON // 2
    lit_counts = jax.random.randint(key_lit, (TLON, TLAT), HALF, BLK + 1)
    dark_counts = jax.random.randint(key_dark, (TLON, TLAT), 0, HALF // 4 + 1)
    counts = jnp.where(dayside, lit_counts, dark_counts)
    counts = jnp.where((relative == 0) & (lat_tiles == 0), BLK, counts)
    counts = jnp.where((relative == TLON // 2) & (lat_tiles == 0), 0, counts)
    return counts.astype(jnp.int32)


def level_of(stream_key, dims, pieces, least, top_value):
    def one(position, shards_of):
        steps = jax.random.uniform(jax.random.fold_in(jax.random.fold_in(stream_key, 6), position), (shards_of,), jnp.float32, least / len(pieces), top_value / len(pieces))
        return jnp.repeat(jnp.exp(steps), dims[position] // shards_of).reshape((-1,) + (1,) * (len(dims) - position - 1))

    level = one(*pieces[0])
    for cut in pieces[1:]:
        level = level * one(*cut)
    return level


def setup_inputs(seed: int = 0) -> dict:
    keys = jax.random.split(jax.random.key(seed), 8)
    return {
        "tracers": jnp.clip(jnp.exp(math.log(2.0) - 2.3025851 * jax.random.uniform(keys[0], (SPECIES, NLON, NLAT, LEV), jnp.float32) ** level_of(keys[0], (SPECIES, NLON, NLAT, LEV), ((1, 8), (2, 4)), -0.2, 0.2)), 0.2, 2.0),
        "kdiff": jnp.clip(jnp.exp(math.log(8.0) - 3.2834143 * jax.random.uniform(keys[1], (NLON, NLAT, LEV), jnp.float32) ** level_of(keys[1], (NLON, NLAT, LEV), ((0, 8), (1, 4)), -0.2, 0.2)), 0.3, 8.0),
        "photolysis": jnp.clip(jnp.exp(math.log(2.0) - 3.6888794 * jax.random.uniform(keys[2], (NLON, NLAT, LEV), jnp.float32) ** level_of(keys[2], (NLON, NLAT, LEV), ((0, 8), (1, 4)), -0.2, 0.2)), 0.05, 2.0),
        "u_wind": jnp.clip(jax.random.uniform(keys[3], (NLON, NLAT, LEV), jnp.float32, -0.24, 0.24) * level_of(keys[3], (NLON, NLAT, LEV), ((0, 8), (1, 4)), -0.4, 0.0), -0.24, 0.24),
        "v_wind": jnp.clip(jax.random.uniform(keys[4], (NLON, NLAT, LEV), jnp.float32, -0.24, 0.24) * level_of(keys[4], (NLON, NLAT, LEV), ((0, 8), (1, 4)), -0.4, 0.0), -0.24, 0.24),
        "day_count": draw_day_count(jax.random.fold_in(keys[7], 71), 0),
        "day_order": jax.vmap(lambda own: jax.random.permutation(own, BLK))(jax.random.split(keys[6], TLON * TLAT)).reshape((TLON, TLAT, BLK)).astype(jnp.int32),
    }


def section_table(sections):
    bvals = [1.0 / 3.0] * 3 + [(j * j + j - 2.0) / (2.0 * j * (j + 1.0)) for j in range(3, sections + 1)]
    scale = 4.0 / (sections * sections + sections - 2.0)
    rows = []
    for j in range(2, sections + 1):
        coef_prev = (2.0 * j - 1.0) / j * bvals[j] / bvals[j - 1]
        coef_back = -(j - 1.0) / j * bvals[j] / bvals[j - 2]
        coef_step = coef_prev * scale
        coef_first = -(1.0 - bvals[j - 1]) * coef_step
        rows.append((coef_prev, coef_back, 1.0 - coef_prev - coef_back, coef_step, coef_first))
    return bvals[1] * scale, rows


def tendency(field, diffusion, photo):
    above = jnp.concatenate([field[..., 1:], field[..., -1:]], axis=-1)
    upward = diffusion * (above - field)
    below = jnp.concatenate([jnp.zeros_like(upward[..., :1]), upward[..., :-1]], axis=-1)
    mixing = upward - below
    ozone, oxygen, nitric, dioxide = field[0], field[1], field[2], field[3]
    titration = ozone * nitric
    split_no2 = 2.0 * photo * dioxide
    split_o3 = 0.25 * photo * ozone
    chemistry = jnp.stack([1.5 * oxygen - titration - split_o3,
                           split_no2 + split_o3 - 1.5 * oxygen,
                           split_no2 - titration,
                           titration - split_no2], axis=0)
    return mixing + 0.5 * chemistry


def column_step(field, diffusion, photo):
    first_coef, table = section_table(SECTIONS)
    start_rate = tendency(field, diffusion, photo)
    previous = field
    current = field + first_coef * start_rate
    for coef_prev, coef_back, coef_base, coef_step, coef_first in table:
        following = (coef_prev * current + coef_back * previous + coef_base * field
                     + coef_step * tendency(current, diffusion, photo) + coef_first * start_rate)
        previous, current = current, following
    return current


def night_step(field):
    ozone, oxygen, nitric = field[0], field[1], field[2]
    titration = ozone * nitric
    change = jnp.stack([1.5 * oxygen - titration, -1.5 * oxygen, -titration, titration], axis=0)
    return field + 0.5 * change


def daylit_columns(day_count, day_order):
    positions = jnp.arange(BLK, dtype=jnp.int32)
    live = positions[None, None, :] < day_count[:, :, None]
    match = day_order[:, :, :, None] == positions[None, None, None, :]
    daylit = jnp.any(match & live[:, :, :, None], axis=2)
    per_column = jnp.repeat(daylit, BCOL, axis=2)
    per_column = per_column.reshape(TLON, TLAT, CLON, CLAT).transpose(0, 2, 1, 3)
    return per_column.reshape(TLON, CLON * NLAT)


def reference(tracers, kdiff, photolysis, u_wind, v_wind, day_count, day_order):
    slabs = jnp.moveaxis(tracers.reshape(SPECIES, TLON, CLON * NLAT, LEV), 1, 0)
    diff_slabs = kdiff.reshape(TLON, CLON * NLAT, LEV)
    photo_slabs = photolysis.reshape(TLON, CLON * NLAT, LEV)
    lit = daylit_columns(day_count, day_order)

    def one_slab(items):
        field, diffusion, photo, mask = items
        return jnp.where(mask[None, :, None], column_step(field, diffusion, photo), night_step(field))

    stepped = lax.map(one_slab, (slabs, diff_slabs, photo_slabs, lit))
    stepped = jnp.moveaxis(stepped, 0, 1).reshape(SPECIES, NLON, NLAT, LEV)

    def advect_one(field):
        east = jnp.maximum(u_wind, 0.0) * field + jnp.minimum(u_wind, 0.0) * jnp.roll(field, -1, axis=0)
        west = jnp.roll(east, 1, axis=0)
        ahead = jnp.concatenate([field[:, 1:], jnp.zeros_like(field[:, :1])], axis=1)
        north = jnp.maximum(v_wind, 0.0) * field + jnp.minimum(v_wind, 0.0) * ahead
        south = jnp.concatenate([jnp.zeros_like(north[:, :1]), north[:, :-1]], axis=1)
        return field - (east - west) - (north - south)

    return lax.map(advect_one, stepped)
```

```python
import jax
import jax.numpy as jnp
from jax import lax
from jax.experimental import pallas as pl
from jax.experimental.pallas import tpu as pltpu
from jax.sharding import PartitionSpec as P

SECTIONS = 12
SUB = 8
FIELDS = 6


def section_table(sections):
    bvals = [1.0 / 3.0] * 3 + [
        (j * j + j - 2.0) / (2.0 * j * (j + 1.0)) for j in range(3, sections + 1)
    ]
    rate = 4.0 / (sections * sections + sections - 2.0)
    scale = [1.0, 1.0]
    for j in range(2, sections + 1):
        scale.append(-(j - 1.0) / j * scale[j - 2])
    lead = [0.0, 0.0] + [
        (2.0 * j - 1.0) / j * scale[j - 1] / scale[j] for j in range(2, sections + 1)
    ]
    return bvals, rate, scale, lead


BVALS, RATE, SCALE, LEAD = section_table(SECTIONS)
HALF = 0.5 * RATE
OXYGEN = 1.5 * HALF


def stage_consts(j):
    b, scale = BVALS[j - 1], SCALE[j - 1]
    rho = (1.0 - b) / (b * scale)
    return LEAD[j], rho, HALF * b * scale, rho * HALF


def rows(i):
    return pl.ds(SUB * i, SUB)


def runs(i, steps):
    return pl.ds(i, SUB, stride=steps + 1)


def sweep(coef, steps, load, titration, finish):
    first, end = load(0), load(steps - 1)
    k_end = coef[0, rows(steps - 1), :]
    f_end = [k_end * (pltpu.roll(n, SUB - 1, axis=0) - c) for n, c in zip(first, end)]
    before = [pltpu.roll(f, 1, axis=0) for f in f_end]
    current = first
    for i in range(steps):
        if i < steps - 1:
            above = load(i + 1)
            k = coef[0, rows(i), :]
            flux = [k * (n - c) for n, c in zip(above, current)]
        else:
            above, flux = None, f_end
        t = titration(i, current)
        gain = [a - b for a, b in zip(flux, before)]
        ozone = (coef[2, rows(i), :] * current[0] + gain[0]) + (
            OXYGEN * (current[3] - current[1]) - t
        )
        dioxide = (coef[1, rows(i), :] * current[1] + gain[1]) + t
        finish(i, [ozone, dioxide, current[2] + gain[2], current[3] + gain[3]])
        current, before = above, flux


def prepare(i, steps, tin, state, coef):
    ozone, oxygen, nitric, dioxide, k, photo = (tin[s, runs(i, steps), :] for s in range(FIELDS))
    k = k * RATE
    if i == steps - 1:
        k = jnp.where(lax.broadcasted_iota(jnp.int32, k.shape, 0) == SUB - 1, 0.0, k)
    split = photo * (2.0 * HALF)
    odd = (ozone + oxygen) + dioxide
    for s, value in enumerate((ozone, dioxide, nitric + dioxide, odd, nitric)):
        state[s, rows(i), :] = value
    for s, value in enumerate((k, 1.0 - split, (1.0 - OXYGEN) - 0.125 * split, ozone * nitric)):
        coef[s, rows(i), :] = value


def conclude(i, steps, tout, state, bufs):
    base, weight = 1.0 - BVALS[SECTIONS], BVALS[SECTIONS] * SCALE[SECTIONS]
    ozone, dioxide, nitrogen, odd = (
        weight * bufs[SECTIONS % 2, s, rows(i), :] + base * state[s, rows(i), :] for s in range(4)
    )
    for s, value in enumerate((ozone, (odd - dioxide) - ozone, nitrogen - dioxide, dioxide)):
        tout[s, runs(i, steps), :] = value


def first_stage(steps, state, bufs, coef, exchange):
    ready = set()

    def load(i):
        if i not in ready:
            ready.add(i)
            exchange(i)
        return [state[s, rows(i), :] for s in range(4)]

    def finish(i, fields):
        for s in range(4):
            bufs[1, s, rows(i), :] = fields[s]

    sweep(coef, steps, load, lambda i, current: HALF * coef[3, rows(i), :], finish)


def later_stage(consts, steps, source, back, target, state, coef):
    lead, rho, kappa, base = consts

    def titration(i, current):
        left = kappa * (current[0] + rho * state[0, rows(i), :])
        right = (current[2] - current[1]) + rho * state[4, rows(i), :]
        return left * right - base * coef[3, rows(i), :]

    def finish(i, fields):
        for s in range(4):
            target[s, rows(i), :] = lead * fields[s] + back[s, rows(i), :]

    sweep(
        coef, steps, lambda i: [source[s, rows(i), :] for s in range(4)], titration, finish
    )


def column_kernel(
    counts, ranks, y, k, p, u, v, mix, lon_tail, lon_head, lat_tail, lat_head,
    raw, tin, tout, state, bufs, coef, wind, table, count, rank, flag, order, sem, wsem, ssem,
):
    species, blocks, cols, levels = y.shape
    lon_cells, lat_cells = u.shape[:2]
    steps = levels // SUB
    for j in range(3, SECTIONS + 1):
        for c, value in enumerate(stage_consts(j)):
            table[j - 3, c] = value

    def fetch(b, _):
        for src, dst in (
            (y.at[:, b], raw.at[pl.ds(0, species), b]),
            (k.at[b], raw.at[species, b]),
            (p.at[b], raw.at[species + 1, b]),
        ):
            pltpu.make_async_copy(src, dst, sem.at[b]).start()
        return 0

    def arrive(n):
        b = order[n]
        whole = raw.at[:, b]
        pltpu.make_async_copy(whole, whole, sem.at[b]).wait()
        return b

    def place(b):
        return pl.ds(pl.multiple_of(b * cols, cols), cols)

    def bring(s, b):
        x = raw[s, b].T
        for g in range(SUB):
            tin[s, pl.ds(g * (steps + 1), steps), :] = x[g * steps : (g + 1) * steps, :]

    def emit(s, b):
        x = jnp.concatenate(
            [tout[s, pl.ds(g * (steps + 1), steps), :] for g in range(SUB)], axis=0
        )
        mix[s, place(b), :] = x.T

    winds = (
        pltpu.make_async_copy(u.at[lon_cells - 1], lon_tail.at[species], wsem.at[0]),
        pltpu.make_async_copy(v.at[:, pl.ds(lat_cells - SUB, SUB)], wind, wsem.at[1]),
    )
    lists = (
        pltpu.make_async_copy(counts, count, ssem.at[0]),
        pltpu.make_async_copy(ranks, rank, ssem.at[1]),
    )
    for copy in lists:
        copy.start()
    lax.fori_loop(0, blocks, fetch, 0)
    for copy in winds:
        copy.start()
    for copy in lists:
        copy.wait()
    lit = count[lax.axis_index("lat"), lax.axis_index("lon")]

    def mark(n, _):
        flag[rank[0, 0, n]] = jnp.where(n < lit, 0, 1)
        return 0

    lax.fori_loop(0, blocks, mark, 0)

    def sort(b, ends):
        first, final = ends
        dark = flag[b]
        order[jnp.where(dark == 0, first, final)] = b
        return first + 1 - dark, final + dark

    lax.fori_loop(0, blocks, sort, (0, lit))

    @pl.when(lit > 0)
    def _():
        start = arrive(0)
        for s in range(FIELDS):
            bring(s, start)

        def turn(n, _):
            @pl.when(n + 1 < lit)
            def _():
                arrive(n + 1)

            coming = order[jnp.minimum(n + 1, lit - 1)]
            leaving = jnp.where(n > 0, order[jnp.maximum(n - 1, 0)], blocks)
            def exchange(i):
                conclude(i, steps, tout, state, bufs)
                prepare(i, steps, tin, state, coef)

            first_stage(steps, state, bufs, coef, exchange)
            bring(FIELDS - 1, coming)
            later_stage(stage_consts(2), steps, bufs.at[1], state, bufs.at[0], state, coef)

            def pair(turn_pair, _):
                bring(turn_pair, coming)
                emit(jnp.minimum(turn_pair, species - 1), leaving)
                for q in range(2):
                    consts = [table[2 * turn_pair + q, c] for c in range(4)]
                    now, other = bufs.at[q], bufs.at[1 - q]
                    later_stage(consts, steps, now, other, other, state, coef)
                return 0

            lax.fori_loop(0, (SECTIONS - 2) // 2, pair, 0)
            return 0

        lax.fori_loop(0, lit, turn, 0)
        for i in range(steps):
            conclude(i, steps, tout, state, bufs)
        for s in range(species):
            emit(s, order[lit - 1])

    def night(n, _):
        b = arrive(n)
        ozone, oxygen, nitric, dioxide = (raw[s, b] for s in range(species))
        t = 0.5 * (ozone * nitric)
        values = (ozone + (0.75 * oxygen - t), oxygen - 0.75 * oxygen, nitric - t, dioxide + t)
        for s, value in enumerate(values):
            mix[s, place(b), :] = value
        return 0

    lax.fori_loop(lit, blocks, night, 0)
    for copy in winds:
        copy.wait()
    for s in range(species):
        lon_head[s] = mix[s, pl.ds(0, lat_cells), :]
        lon_tail[s] = mix[s, pl.ds((lon_cells - 1) * lat_cells, lat_cells), :]
        for i in range(lon_cells // SUB):
            start = i * SUB * lat_cells
            lat_head[s, rows(i), :] = mix[s, pl.ds(start, SUB, stride=lat_cells), :]
            lat_tail[s, rows(i), :] = mix[s, pl.ds(start + lat_cells - 1, SUB, stride=lat_cells), :]
    flat = wind.reshape(lon_cells * SUB, levels)
    for i in range(lon_cells // SUB):
        lat_tail[species, rows(i), :] = flat[pl.ds(i * SUB * SUB + SUB - 1, SUB, stride=SUB), :]


def buffer(*dims):
    return pltpu.VMEM(dims, jnp.float32)


ANYWHERE = pl.BlockSpec(memory_space=pl.ANY)
VECTORS = pl.BlockSpec(memory_space=pltpu.VMEM)


def in_hbm(x):
    return pltpu.with_memory_space_constraint(x, pltpu.HBM)


def in_vmem(x):
    return pltpu.with_memory_space_constraint(x, pltpu.VMEM)


def column_pass(count, order, tracers, kdiff, photolysis, u_wind, v_wind):
    species, lon_cells, lat_cells, levels = tracers.shape
    blocks = order.shape[2]
    cols = lon_cells * lat_cells // blocks
    return pl.pallas_call(
        column_kernel,
        in_specs=[ANYWHERE] * 7,
        out_specs=[VECTORS] * 5,
        out_shape=[
            buffer(species, (blocks + 1) * cols, levels),
            buffer(species + 1, lat_cells, levels),
            buffer(species, lat_cells, levels),
            buffer(species + 1, lon_cells, levels),
            buffer(species, lon_cells, levels),
        ],
        scratch_shapes=[
            buffer(FIELDS, blocks, cols, levels),
            buffer(FIELDS, levels + SUB, cols),
            buffer(species, levels + SUB, cols),
            buffer(species + 1, levels, cols),
            buffer(2, species, levels, cols),
            buffer(4, levels, cols),
            buffer(lon_cells, SUB, levels),
            pltpu.SMEM((SECTIONS - 2, 4), jnp.float32),
            pltpu.SMEM(count.shape, jnp.int32),
            pltpu.SMEM(order.shape, jnp.int32),
            pltpu.SMEM((blocks,), jnp.int32),
            pltpu.SMEM((blocks,), jnp.int32),
            pltpu.SemaphoreType.DMA((blocks,)),
            pltpu.SemaphoreType.DMA((2,)),
            pltpu.SemaphoreType.DMA((2,)),
        ],
        compiler_params=pltpu.CompilerParams(vmem_limit_bytes=24 << 20),
        name="columns",
    )(
        in_hbm(count),
        in_hbm(order),
        in_hbm(tracers.reshape(species, blocks, cols, levels)),
        in_hbm(kdiff.reshape(blocks, cols, levels)),
        in_hbm(photolysis.reshape(blocks, cols, levels)),
        in_hbm(u_wind),
        in_hbm(v_wind),
    )


def transport_kernel(
    mix, u, v, out, lon_rim, lat_rim, east_flux, north_flux, stage, sem,
):
    lon_cells, lat_cells, levels = u.shape
    species = out.shape[0]
    tiles = lat_cells // SUB
    zero = jnp.zeros((SUB, levels), jnp.float32)
    row = lax.broadcasted_iota(jnp.int32, (SUB, levels), 0)
    for s in range(species):
        for q in range(2):
            north_flux[q, s, rows(0), :] = zero
        for t in range(tiles):
            east_flux[s, rows(t), :] = zero

    def line(i, q, last, put):
        base = pl.multiple_of(i * lat_cells, SUB)
        for t in range(tiles):
            wu, wv = u[i, rows(t), :], v[i, rows(t), :]
            east_going, north_going = wu > 0.0, wv > 0.0
            for s in range(species):
                here = mix[s, pl.ds(base + t * SUB, SUB), :]
                donor = 0.0 if last else mix[s, pl.ds(base + lat_cells + t * SUB, SUB), :]
                x_flux = wu * jnp.where(east_going, here, donor)
                if t < tiles - 1:
                    ahead = mix[s, pl.ds(base + t * SUB + 1, SUB), :]
                else:
                    ahead = jnp.where(row < SUB - 1, pltpu.roll(here, SUB - 1, axis=0), 0.0)
                y_flux = wv * jnp.where(north_going, here, ahead)
                north_flux[q, s, rows(t + 1), :] = y_flux
                x_loss = x_flux - east_flux[s, rows(t), :]
                east_flux[s, rows(t), :] = x_flux
                y_loss = y_flux - north_flux[q, s, pl.ds(t * SUB + SUB - 1, SUB), :]
                put(s, t, (here - x_loss) - y_loss)

    def rim_row(side):
        def put(s, t, value):
            lon_rim[s, side, rows(t), :] = value

        return put

    def inner_row(i):
        def put(s, t, value):
            if 0 < t < tiles - 1:
                stage[s, i - 1, rows(t - 1), :] = value
            else:
                lat_rim[s, min(t, 1), i - 1] = value

        return put

    inner = pl.ds(SUB, lat_cells - 2 * SUB)

    def ship(i, count):
        return pltpu.make_async_copy(
            stage.at[:, pl.ds(i - 1, count)], out.at[:, pl.ds(i, count), inner], sem.at[0]
        )

    line(0, 0, False, rim_row(0))

    def two(n, _):
        i = 1 + 2 * n
        line(i, 0, False, inner_row(i))
        line(i + 1, 1, False, inner_row(i + 1))
        ship(i, 2).start()
        return 0

    lax.fori_loop(0, (lon_cells - 2) // 2, two, 0)
    line(lon_cells - 1, 0, True, rim_row(1))
    ship(1, lon_cells - 2).wait()


def transport(mix, u_wind, v_wind, species):
    lon_cells, lat_cells, levels = u_wind.shape
    return pl.pallas_call(
        transport_kernel,
        in_specs=[VECTORS] * 3,
        out_specs=[ANYWHERE] + [VECTORS] * 2,
        out_shape=[
            pltpu.HBM((species, lon_cells, lat_cells, levels), jnp.float32),
            buffer(species, 2, lat_cells, levels),
            buffer(species, 2, lon_cells - 2, SUB, levels),
        ],
        scratch_shapes=[
            buffer(species, lat_cells, levels),
            buffer(2, species, lat_cells + SUB, levels),
            buffer(species, lon_cells - 2, lat_cells - 2 * SUB, levels),
            pltpu.SemaphoreType.DMA((1,)),
        ],
        compiler_params=pltpu.CompilerParams(vmem_limit_bytes=12 << 20),
        name="transport",
    )(in_vmem(mix), in_vmem(u_wind), in_vmem(v_wind))


def rim_kernel(
    partial, lon_rim, lat_rim, west, east, south, north, lon_tail, lon_head, lat_tail, lat_head,
    out, lon_new, lat_new, sem,
):
    species, lon_cells, lat_cells, levels = out.shape
    inner = lon_cells - 2
    wind = west[species]
    wind_out = lon_tail[species]
    place = lax.axis_index("lat")
    south_wind = jnp.where(place > 0, south[species], 0.0)
    north_wind = jnp.where(place < lax.axis_size("lat") - 1, lat_tail[species], 0.0)
    for s in range(species):
        inflow = jnp.maximum(wind, 0.0) * west[s] + jnp.minimum(wind, 0.0) * lon_head[s]
        lon_new[s, 0] = lon_rim[s, 0] + inflow
        lon_new[s, 1] = lon_rim[s, 1] - jnp.minimum(wind_out, 0.0) * east[s]
        first = jnp.maximum(south_wind, 0.0) * south[s] + jnp.minimum(south_wind, 0.0) * lat_head[s]
        final = jnp.minimum(north_wind, 0.0) * north[s]
        for side, (at, change) in enumerate(((0, first), (lat_cells - 1, -final))):
            lat_new[s, side] = lat_rim[s, side]
            for q, i in ((0, 0), (1, lon_cells - 1)):
                lon_new[s, q, pl.ds(at, 1), :] = lon_new[s, q, pl.ds(at, 1), :] + change[i : i + 1, :]
            for i in range(inner):
                spot = (s, side, i, pl.ds(at % SUB, 1))
                lat_new[spot] = lat_new[spot] + change[i + 1 : i + 2, :]
    copies = [
        pltpu.make_async_copy(lon_new.at[:, q], out.at[:, i], sem.at[q])
        for q, i in ((0, 0), (1, lon_cells - 1))
    ] + [
        pltpu.make_async_copy(
            lat_new.at[:, q], out.at[:, pl.ds(1, inner), pl.ds(start, SUB)], sem.at[2 + q]
        )
        for q, start in ((0, 0), (1, lat_cells - SUB))
    ]
    for copy in copies:
        copy.start()
    for copy in copies:
        copy.wait()


def rim_pass(partial, rims, halos, edges):
    species, lon_cells, lat_cells, levels = partial.shape
    return pl.pallas_call(
        rim_kernel,
        in_specs=[ANYWHERE] + [VECTORS] * 10,
        out_specs=ANYWHERE,
        out_shape=pltpu.HBM(partial.shape, jnp.float32),
        input_output_aliases={0: 0},
        scratch_shapes=[
            buffer(species, 2, lat_cells, levels),
            buffer(species, 2, lon_cells - 2, SUB, levels),
            pltpu.SemaphoreType.DMA((4,)),
        ],
        compiler_params=pltpu.CompilerParams(vmem_limit_bytes=12 << 20),
        name="rim",
    )(in_hbm(partial), *(in_vmem(x) for x in (*rims, *halos, *edges)))


def body(tracers, kdiff, photolysis, u_wind, v_wind, day_count, day_order):
    mix, *edges = column_pass(
        day_count.T, day_order, tracers, kdiff, photolysis, u_wind, v_wind
    )
    lon_tail, lon_head, lat_tail, lat_head = edges

    def shift(edge, axis, step):
        size = lax.axis_size(axis)
        return lax.ppermute(edge, axis, [(i, (i + step) % size) for i in range(size)])

    halos = (
        shift(lon_tail, "lon", 1),
        shift(lon_head, "lon", -1),
        shift(lat_tail, "lat", 1),
        shift(lat_head, "lat", -1),
    )
    partial, *rims = transport(mix, u_wind, v_wind, tracers.shape[0])
    return rim_pass(partial, rims, halos, edges)


def solution(mesh):
    return jax.shard_map(
        body,
        mesh=mesh,
        in_specs=(
            P(None, "lon", "lat", None),
            P("lon", "lat", None),
            P("lon", "lat", None),
            P("lon", "lat", None),
            P("lon", "lat", None),
            P(),
            P("lon", "lat", None),
        ),
        out_specs=P(None, "lon", "lat", None),
        check_vma=False,
    )
```

```python
import jax
import jax.numpy as jnp
from jax import lax
from jax.experimental import pallas as pl
from jax.experimental.pallas import tpu as pltpu
from jax.sharding import PartitionSpec as P

SECTIONS = 12
SUB = 8
FIELDS = 6


def section_table(sections):
    bvals = [1.0 / 3.0] * 3 + [
        (j * j + j - 2.0) / (2.0 * j * (j + 1.0)) for j in range(3, sections + 1)
    ]
    rate = 4.0 / (sections * sections + sections - 2.0)
    scale = [1.0, 1.0]
    for j in range(2, sections + 1):
        scale.append(-(j - 1.0) / j * scale[j - 2])
    lead = [0.0, 0.0] + [
        (2.0 * j - 1.0) / j * scale[j - 1] / scale[j] for j in range(2, sections + 1)
    ]
    return bvals, rate, scale, lead


BVALS, RATE, SCALE, LEAD = section_table(SECTIONS)
HALF = 0.5 * RATE
OXYGEN = 1.5 * HALF


def stage_consts(j):
    b, scale = BVALS[j - 1], SCALE[j - 1]
    rho = (1.0 - b) / (b * scale)
    return LEAD[j], rho, HALF * b * scale, rho * HALF


def rows(i):
    return pl.ds(SUB * i, SUB)


def runs(i, steps):
    return pl.ds(i, SUB, stride=steps + 1)


def sweep(coef, steps, load, titration, finish):
    first, end = load(0), load(steps - 1)
    k_end = coef[0, rows(steps - 1), :]
    f_end = [k_end * (pltpu.roll(n, SUB - 1, axis=0) - c) for n, c in zip(first, end)]
    before = [pltpu.roll(f, 1, axis=0) for f in f_end]
    current = first
    for i in range(steps):
        if i < steps - 1:
            above = load(i + 1)
            k = coef[0, rows(i), :]
            flux = [k * (n - c) for n, c in zip(above, current)]
        else:
            above, flux = None, f_end
        t = titration(i, current)
        gain = [a - b for a, b in zip(flux, before)]
        ozone = (coef[2, rows(i), :] * current[0] + gain[0]) + (
            OXYGEN * (current[3] - current[1]) - t
        )
        dioxide = (coef[1, rows(i), :] * current[1] + gain[1]) + t
        finish(i, [ozone, dioxide, current[2] + gain[2], current[3] + gain[3]])
        current, before = above, flux


def prepare(i, steps, tin, state, coef):
    ozone, oxygen, nitric, dioxide, k, photo = (tin[s, runs(i, steps), :] for s in range(FIELDS))
    k = k * RATE
    if i == steps - 1:
        k = jnp.where(lax.broadcasted_iota(jnp.int32, k.shape, 0) == SUB - 1, 0.0, k)
    split = photo * (2.0 * HALF)
    odd = (ozone + oxygen) + dioxide
    for s, value in enumerate((ozone, dioxide, nitric + dioxide, odd, nitric)):
        state[s, rows(i), :] = value
    for s, value in enumerate((k, 1.0 - split, (1.0 - OXYGEN) - 0.125 * split, ozone * nitric)):
        coef[s, rows(i), :] = value


def conclude(i, steps, tout, state, bufs):
    base, weight = 1.0 - BVALS[SECTIONS], BVALS[SECTIONS] * SCALE[SECTIONS]
    ozone, dioxide, nitrogen, odd = (
        weight * bufs[SECTIONS % 2, s, rows(i), :] + base * state[s, rows(i), :] for s in range(4)
    )
    for s, value in enumerate((ozone, (odd - dioxide) - ozone, nitrogen - dioxide, dioxide)):
        tout[s, runs(i, steps), :] = value


def first_stage(steps, state, bufs, coef, exchange):
    ready = set()

    def load(i):
        if i not in ready:
            ready.add(i)
            exchange(i)
        return [state[s, rows(i), :] for s in range(4)]

    def finish(i, fields):
        for s in range(4):
            bufs[1, s, rows(i), :] = fields[s]

    sweep(coef, steps, load, lambda i, current: HALF * coef[3, rows(i), :], finish)


def later_stage(consts, steps, source, back, target, state, coef):
    lead, rho, kappa, base = consts

    def titration(i, current):
        left = kappa * (current[0] + rho * state[0, rows(i), :])
        right = (current[2] - current[1]) + rho * state[4, rows(i), :]
        return left * right - base * coef[3, rows(i), :]

    def finish(i, fields):
        for s in range(4):
            target[s, rows(i), :] = lead * fields[s] + back[s, rows(i), :]

    sweep(
        coef, steps, lambda i: [source[s, rows(i), :] for s in range(4)], titration, finish
    )


def column_kernel(
    counts, ranks, y, k, p, u, v, mix, lon_tail, lon_head, lat_tail, lat_head,
    raw, tin, tout, state, bufs, coef, wind, table, count, rank, flag, order, sem, wsem, ssem,
):
    species, blocks, cols, levels = y.shape
    lon_cells, lat_cells = u.shape[:2]
    steps = levels // SUB
    for j in range(3, SECTIONS + 1):
        for c, value in enumerate(stage_consts(j)):
            table[j - 3, c] = value

    def fetch(b, _):
        for src, dst in (
            (y.at[:, b], raw.at[pl.ds(0, species), b]),
            (k.at[b], raw.at[species, b]),
            (p.at[b], raw.at[species + 1, b]),
        ):
            pltpu.make_async_copy(src, dst, sem.at[b]).start()
        return 0

    def arrive(n):
        b = order[n]
        whole = raw.at[:, b]
        pltpu.make_async_copy(whole, whole, sem.at[b]).wait()
        return b

    def place(b):
        return pl.ds(pl.multiple_of(b * cols, cols), cols)

    def bring(s, b):
        x = raw[s, b].T
        for g in range(SUB):
            tin[s, pl.ds(g * (steps + 1), steps), :] = x[g * steps : (g + 1) * steps, :]

    def emit(s, b):
        x = jnp.concatenate(
            [tout[s, pl.ds(g * (steps + 1), steps), :] for g in range(SUB)], axis=0
        )
        mix[s, place(b), :] = x.T

    winds = (
        pltpu.make_async_copy(u.at[lon_cells - 1], lon_tail.at[species], wsem.at[0]),
        pltpu.make_async_copy(v.at[:, pl.ds(lat_cells - SUB, SUB)], wind, wsem.at[1]),
    )
    lists = (
        pltpu.make_async_copy(counts, count, ssem.at[0]),
        pltpu.make_async_copy(ranks, rank, ssem.at[1]),
    )
    for copy in lists:
        copy.start()
    lax.fori_loop(0, blocks, fetch, 0)
    for copy in winds:
        copy.start()
    for copy in lists:
        copy.wait()
    lit = count[lax.axis_index("lat"), lax.axis_index("lon")]

    def mark(n, _):
        flag[rank[0, 0, n]] = jnp.where(n < lit, 0, 1)
        return 0

    lax.fori_loop(0, blocks, mark, 0)

    def sort(b, ends):
        first, final = ends
        dark = flag[b]
        order[jnp.where(dark == 0, first, final)] = b
        return first + 1 - dark, final + dark

    lax.fori_loop(0, blocks, sort, (0, lit))

    @pl.when(lit > 0)
    def _():
        start = arrive(0)
        for s in range(FIELDS):
            bring(s, start)

        def turn(n, _):
            @pl.when(n + 1 < lit)
            def _():
                arrive(n + 1)

            coming = order[jnp.minimum(n + 1, lit - 1)]
            leaving = jnp.where(n > 0, order[jnp.maximum(n - 1, 0)], blocks)
            def exchange(i):
                conclude(i, steps, tout, state, bufs)
                prepare(i, steps, tin, state, coef)

            first_stage(steps, state, bufs, coef, exchange)
            bring(FIELDS - 1, coming)
            later_stage(stage_consts(2), steps, bufs.at[1], state, bufs.at[0], state, coef)

            def pair(turn_pair, _):
                bring(turn_pair, coming)
                emit(jnp.minimum(turn_pair, species - 1), leaving)
                for q in range(2):
                    consts = [table[2 * turn_pair + q, c] for c in range(4)]
                    now, other = bufs.at[q], bufs.at[1 - q]
                    later_stage(consts, steps, now, other, other, state, coef)
                return 0

            lax.fori_loop(0, (SECTIONS - 2) // 2, pair, 0)
            return 0

        lax.fori_loop(0, lit, turn, 0)
        for i in range(steps):
            conclude(i, steps, tout, state, bufs)
        for s in range(species):
            emit(s, order[lit - 1])

    def night(n, _):
        b = arrive(n)
        ozone, oxygen, nitric, dioxide = (raw[s, b] for s in range(species))
        t = 0.5 * (ozone * nitric)
        values = (ozone + (0.75 * oxygen - t), oxygen - 0.75 * oxygen, nitric - t, dioxide + t)
        for s, value in enumerate(values):
            mix[s, place(b), :] = value
        return 0

    lax.fori_loop(lit, blocks, night, 0)
    for copy in winds:
        copy.wait()
    for s in range(species):
        lon_head[s] = mix[s, pl.ds(0, lat_cells), :]
        lon_tail[s] = mix[s, pl.ds((lon_cells - 1) * lat_cells, lat_cells), :]
        for i in range(lon_cells // SUB):
            start = i * SUB * lat_cells
            lat_head[s, rows(i), :] = mix[s, pl.ds(start, SUB, stride=lat_cells), :]
            lat_tail[s, rows(i), :] = mix[s, pl.ds(start + lat_cells - 1, SUB, stride=lat_cells), :]
    flat = wind.reshape(lon_cells * SUB, levels)
    for i in range(lon_cells // SUB):
        lat_tail[species, rows(i), :] = flat[pl.ds(i * SUB * SUB + SUB - 1, SUB, stride=SUB), :]


def buffer(*dims):
    return pltpu.VMEM(dims, jnp.float32)


ANYWHERE = pl.BlockSpec(memory_space=pl.ANY)
VECTORS = pl.BlockSpec(memory_space=pltpu.VMEM)


def in_hbm(x):
    return pltpu.with_memory_space_constraint(x, pltpu.HBM)


def in_vmem(x):
    return pltpu.with_memory_space_constraint(x, pltpu.VMEM)


def column_pass(count, order, tracers, kdiff, photolysis, u_wind, v_wind):
    species, lon_cells, lat_cells, levels = tracers.shape
    blocks = order.shape[2]
    cols = lon_cells * lat_cells // blocks
    return pl.pallas_call(
        column_kernel,
        in_specs=[ANYWHERE] * 7,
        out_specs=[VECTORS] * 5,
        out_shape=[
            buffer(species, (blocks + 1) * cols, levels),
            buffer(species + 1, lat_cells, levels),
            buffer(species, lat_cells, levels),
            buffer(species + 1, lon_cells, levels),
            buffer(species, lon_cells, levels),
        ],
        scratch_shapes=[
            buffer(FIELDS, blocks, cols, levels),
            buffer(FIELDS, levels + SUB, cols),
            buffer(species, levels + SUB, cols),
            buffer(species + 1, levels, cols),
            buffer(2, species, levels, cols),
            buffer(4, levels, cols),
            buffer(lon_cells, SUB, levels),
            pltpu.SMEM((SECTIONS - 2, 4), jnp.float32),
            pltpu.SMEM(count.shape, jnp.int32),
            pltpu.SMEM(order.shape, jnp.int32),
            pltpu.SMEM((blocks,), jnp.int32),
            pltpu.SMEM((blocks,), jnp.int32),
            pltpu.SemaphoreType.DMA((blocks,)),
            pltpu.SemaphoreType.DMA((2,)),
            pltpu.SemaphoreType.DMA((2,)),
        ],
        compiler_params=pltpu.CompilerParams(vmem_limit_bytes=24 << 20),
        name="columns",
    )(
        in_hbm(count),
        in_hbm(order),
        in_hbm(tracers.reshape(species, blocks, cols, levels)),
        in_hbm(kdiff.reshape(blocks, cols, levels)),
        in_hbm(photolysis.reshape(blocks, cols, levels)),
        in_hbm(u_wind),
        in_hbm(v_wind),
    )


def transport_kernel(
    mix, u, v, out, lon_rim, lat_rim, east_flux, north_flux, stage, sem,
):
    lon_cells, lat_cells, levels = u.shape
    species = out.shape[0]
    tiles = lat_cells // SUB
    zero = jnp.zeros((SUB, levels), jnp.float32)
    row = lax.broadcasted_iota(jnp.int32, (SUB, levels), 0)
    for s in range(species):
        for q in range(2):
            north_flux[q, s, rows(0), :] = zero
        for t in range(tiles):
            east_flux[s, rows(t), :] = zero

    def line(i, q, last, put):
        base = pl.multiple_of(i * lat_cells, SUB)
        for t in range(tiles):
            wu, wv = u[i, rows(t), :], v[i, rows(t), :]
            east_going, north_going = wu > 0.0, wv > 0.0
            for s in range(species):
                here = mix[s, pl.ds(base + t * SUB, SUB), :]
                donor = 0.0 if last else mix[s, pl.ds(base + lat_cells + t * SUB, SUB), :]
                x_flux = wu * jnp.where(east_going, here, donor)
                if t < tiles - 1:
                    ahead = mix[s, pl.ds(base + t * SUB + 1, SUB), :]
                else:
                    ahead = jnp.where(row < SUB - 1, pltpu.roll(here, SUB - 1, axis=0), 0.0)
                y_flux = wv * jnp.where(north_going, here, ahead)
                north_flux[q, s, rows(t + 1), :] = y_flux
                x_loss = x_flux - east_flux[s, rows(t), :]
                east_flux[s, rows(t), :] = x_flux
                y_loss = y_flux - north_flux[q, s, pl.ds(t * SUB + SUB - 1, SUB), :]
                put(s, t, (here - x_loss) - y_loss)

    def rim_row(side):
        def put(s, t, value):
            lon_rim[s, side, rows(t), :] = value

        return put

    def inner_row(i):
        def put(s, t, value):
            if 0 < t < tiles - 1:
                stage[s, i - 1, rows(t - 1), :] = value
            else:
                lat_rim[s, min(t, 1), i - 1] = value

        return put

    inner = pl.ds(SUB, lat_cells - 2 * SUB)

    def ship(i, count):
        return pltpu.make_async_copy(
            stage.at[:, pl.ds(i - 1, count)], out.at[:, pl.ds(i, count), inner], sem.at[0]
        )

    line(0, 0, False, rim_row(0))

    def two(n, _):
        i = 1 + 2 * n
        line(i, 0, False, inner_row(i))
        line(i + 1, 1, False, inner_row(i + 1))
        ship(i, 2).start()
        return 0

    lax.fori_loop(0, (lon_cells - 2) // 2, two, 0)
    line(lon_cells - 1, 0, True, rim_row(1))
    ship(1, lon_cells - 2).wait()


def transport(mix, u_wind, v_wind, species):
    lon_cells, lat_cells, levels = u_wind.shape
    return pl.pallas_call(
        transport_kernel,
        in_specs=[VECTORS] * 3,
        out_specs=[ANYWHERE] + [VECTORS] * 2,
        out_shape=[
            pltpu.HBM((species, lon_cells, lat_cells, levels), jnp.float32),
            buffer(species, 2, lat_cells, levels),
            buffer(species, 2, lon_cells - 2, SUB, levels),
        ],
        scratch_shapes=[
            buffer(species, lat_cells, levels),
            buffer(2, species, lat_cells + SUB, levels),
            buffer(species, lon_cells - 2, lat_cells - 2 * SUB, levels),
            pltpu.SemaphoreType.DMA((1,)),
        ],
        compiler_params=pltpu.CompilerParams(vmem_limit_bytes=12 << 20),
        name="transport",
    )(in_vmem(mix), in_vmem(u_wind), in_vmem(v_wind))


def rim_kernel(
    partial, lon_rim, lat_rim, south, north, west, east, lon_tail, lon_head, lat_tail, lat_head,
    out, lon_new, lat_new, sem,
):
    species, lon_cells, lat_cells, levels = out.shape
    inner = lon_cells - 2
    wind = west[species]
    wind_out = jnp.minimum(lon_tail[species], 0.0)
    place = lax.axis_index("lat")
    south_wind = jnp.where(place > 0, south[species], 0.0)
    beyond = place < lax.axis_size("lat") - 1
    north_wind = jnp.where(beyond, jnp.minimum(lat_tail[species], 0.0), 0.0)
    copies = []
    for s in range(species):
        first = south_wind * jnp.where(south_wind > 0.0, south[s], lat_head[s])
        changes = (0, first), (lat_cells - 1, -(north_wind * north[s]))
        lon_new[s, 0] = lon_rim[s, 0] + wind * jnp.where(wind > 0.0, west[s], lon_head[s])
        lon_new[s, 1] = lon_rim[s, 1] - wind_out * east[s]
        for side, (at, change) in enumerate(changes):
            for q, i in ((0, 0), (1, lon_cells - 1)):
                lon_new[s, q, pl.ds(at, 1), :] = lon_new[s, q, pl.ds(at, 1), :] + change[i : i + 1, :]
            for i in range(inner):
                edge = (s, side, i, pl.ds(at % SUB, 1))
                rest = (s, side, i, pl.ds(1 - side, SUB - 1))
                lat_new[rest] = lat_rim[rest]
                lat_new[edge] = lat_rim[edge] + change[i + 1 : i + 2, :]
        for side, (i, start) in enumerate(((0, 0), (lon_cells - 1, lat_cells - SUB))):
            copies += [
                pltpu.make_async_copy(lon_new.at[s, side], out.at[s, i], sem.at[0, side, s]),
                pltpu.make_async_copy(
                    lat_new.at[s, side],
                    out.at[s, pl.ds(1, inner), pl.ds(start, SUB)],
                    sem.at[1, side, s],
                ),
            ]
        for copy in copies[-4:]:
            copy.start()
    for copy in copies:
        copy.wait()


def rim_pass(partial, rims, halos, edges):
    species, lon_cells, lat_cells, levels = partial.shape
    return pl.pallas_call(
        rim_kernel,
        in_specs=[ANYWHERE] + [VECTORS] * 10,
        out_specs=ANYWHERE,
        out_shape=pltpu.HBM(partial.shape, jnp.float32),
        input_output_aliases={0: 0},
        scratch_shapes=[
            buffer(species, 2, lat_cells, levels),
            buffer(species, 2, lon_cells - 2, SUB, levels),
            pltpu.SemaphoreType.DMA((2, 2, species)),
        ],
        compiler_params=pltpu.CompilerParams(vmem_limit_bytes=12 << 20),
        name="rim",
    )(in_hbm(partial), *(in_vmem(x) for x in (*rims, *halos, *edges)))


def body(tracers, kdiff, photolysis, u_wind, v_wind, day_count, day_order):
    mix, *edges = column_pass(
        day_count.T, day_order, tracers, kdiff, photolysis, u_wind, v_wind
    )
    lon_tail, lon_head, lat_tail, lat_head = edges

    def shift(edge, axis, step):
        size = lax.axis_size(axis)
        return lax.ppermute(edge, axis, [(i, (i + step) % size) for i in range(size)])

    south, north = shift(lat_tail, "lat", 1), shift(lat_head, "lat", -1)
    halos = (south, north, shift(lon_tail, "lon", 1), shift(lon_head, "lon", -1))
    partial, *rims = transport(mix, u_wind, v_wind, tracers.shape[0])
    return rim_pass(partial, rims, halos, edges)


def solution(mesh):
    return jax.shard_map(
        body,
        mesh=mesh,
        in_specs=(
            P(None, "lon", "lat", None),
            P("lon", "lat", None),
            P("lon", "lat", None),
            P("lon", "lat", None),
            P("lon", "lat", None),
            P(),
            P("lon", "lat", None),
        ),
        out_specs=P(None, "lon", "lat", None),
        check_vma=False,
    )
```

```python
import math

import jax
import jax.numpy as jnp
from jax import lax
from jax.experimental import pallas as pl
from jax.experimental.pallas import tpu as pltpu
from jax.sharding import PartitionSpec as P

SECTIONS = 12
SUB = 8
FIELDS = 6
ROWS = 4
COPY = 2


def section_table(sections):
    bvals = [1.0 / 3.0] * 3 + [
        (j * j + j - 2.0) / (2.0 * j * (j + 1.0)) for j in range(3, sections + 1)
    ]
    rate = 4.0 / (sections * sections + sections - 2.0)
    scale = [1.0, 1.0]
    for j in range(2, sections + 1):
        scale.append(-(j - 1.0) / j * scale[j - 2])
    lead = [0.0, 0.0] + [
        (2.0 * j - 1.0) / j * scale[j - 1] / scale[j] for j in range(2, sections + 1)
    ]
    return bvals, rate, scale, lead


BVALS, RATE, SCALE, LEAD = section_table(SECTIONS)
HALF = 0.5 * RATE
OXYGEN = 1.5 * HALF


def stage_consts(j):
    b, scale = BVALS[j - 1], SCALE[j - 1]
    rho = (1.0 - b) / (b * scale)
    return LEAD[j], rho, HALF * b * scale, rho * HALF


def rows(i):
    return pl.ds(SUB * i, SUB)


def runs(i, steps):
    return pl.ds(i, SUB, stride=steps + 1)


def sweep(coef, steps, load, titration, finish):
    first, end = load(0), load(steps - 1)
    k_end = coef[0, rows(steps - 1), :]
    f_end = [k_end * (pltpu.roll(n, SUB - 1, axis=0) - c) for n, c in zip(first, end)]
    before = [pltpu.roll(f, 1, axis=0) for f in f_end]
    current = first
    for i in range(steps):
        if i < steps - 1:
            above = load(i + 1)
            k = coef[0, rows(i), :]
            flux = [k * (n - c) for n, c in zip(above, current)]
        else:
            above, flux = None, f_end
        t = titration(i, current)
        gain = [a - b for a, b in zip(flux, before)]
        ozone = (coef[2, rows(i), :] * current[0] + gain[0]) + (
            OXYGEN * (current[3] - current[1]) - t
        )
        dioxide = (coef[1, rows(i), :] * current[1] + gain[1]) + t
        finish(i, [ozone, dioxide, current[2] + gain[2], current[3] + gain[3]])
        current, before = above, flux


def prepare(i, steps, tin, state, coef):
    ozone, oxygen, nitric, dioxide, k, photo = (tin[s, runs(i, steps), :] for s in range(FIELDS))
    k = k * RATE
    if i == steps - 1:
        k = jnp.where(lax.broadcasted_iota(jnp.int32, k.shape, 0) == SUB - 1, 0.0, k)
    split = photo * (2.0 * HALF)
    odd = (ozone + oxygen) + dioxide
    for s, value in enumerate((ozone, dioxide, nitric + dioxide, odd, nitric)):
        state[s, rows(i), :] = value
    for s, value in enumerate((k, 1.0 - split, (1.0 - OXYGEN) - 0.125 * split, ozone * nitric)):
        coef[s, rows(i), :] = value


def conclude(i, steps, tout, state, bufs):
    base, weight = 1.0 - BVALS[SECTIONS], BVALS[SECTIONS] * SCALE[SECTIONS]
    ozone, dioxide, nitrogen, odd = (
        weight * bufs[SECTIONS % 2, s, rows(i), :] + base * state[s, rows(i), :] for s in range(4)
    )
    for s, value in enumerate((ozone, (odd - dioxide) - ozone, nitrogen - dioxide, dioxide)):
        tout[s, runs(i, steps), :] = value


def first_stage(steps, state, bufs, coef, exchange):
    ready = set()

    def load(i):
        if i not in ready:
            ready.add(i)
            exchange(i)
        return [state[s, rows(i), :] for s in range(4)]

    def finish(i, fields):
        for s in range(4):
            bufs[1, s, rows(i), :] = fields[s]

    sweep(coef, steps, load, lambda i, current: HALF * coef[3, rows(i), :], finish)


def later_stage(consts, steps, source, back, target, state, coef):
    lead, rho, kappa, base = consts

    def titration(i, current):
        left = kappa * (current[0] + rho * state[0, rows(i), :])
        right = (current[2] - current[1]) + rho * state[4, rows(i), :]
        return left * right - base * coef[3, rows(i), :]

    def finish(i, fields):
        for s in range(4):
            target[s, rows(i), :] = lead * fields[s] + back[s, rows(i), :]

    sweep(
        coef, steps, lambda i: [source[s, rows(i), :] for s in range(4)], titration, finish
    )


def column_kernel(
    counts, ranks, y, k, p, u, v, mix, lon_tail, lon_head, lat_tail, lat_head,
    raw, tin, tout, state, bufs, coef, wind, table, count, rank, flag, order, got, sem, wsem, ssem,
):
    species, blocks, cols, levels = y.shape
    lon_cells, lat_cells = u.shape[:2]
    steps = levels // SUB
    for j in range(3, SECTIONS + 1):
        for c, value in enumerate(stage_consts(j)):
            table[j - 3, c] = value

    span = blocks // sem.shape[0]

    def fetch(c, _):
        here = pl.ds(c * span, span)
        for src, dst in (
            (y.at[:, here], raw.at[pl.ds(0, species), here]),
            (k.at[here], raw.at[species, here]),
            (p.at[here], raw.at[species + 1, here]),
        ):
            pltpu.make_async_copy(src, dst, sem.at[c]).start()
        got[c] = 0
        return 0

    def arrive(n):
        b = order[n]
        c = lax.div(b, span)

        @pl.when(got[c] == 0)
        def _():
            whole = raw.at[:, pl.ds(c * span, span)]
            pltpu.make_async_copy(whole, whole, sem.at[c]).wait()
            got[c] = 1

        return b

    def place(b):
        return pl.ds(pl.multiple_of(b * cols, cols), cols)

    def bring(s, b):
        x = raw[s, b].T
        for g in range(SUB):
            tin[s, pl.ds(g * (steps + 1), steps), :] = x[g * steps : (g + 1) * steps, :]

    def emit(s, b):
        x = jnp.concatenate(
            [tout[s, pl.ds(g * (steps + 1), steps), :] for g in range(SUB)], axis=0
        )
        mix[s, place(b), :] = x.T

    winds = (
        pltpu.make_async_copy(u.at[lon_cells - 1], lon_tail.at[species], wsem.at[0]),
        pltpu.make_async_copy(v.at[:, pl.ds(lat_cells - SUB, SUB)], wind, wsem.at[1]),
    )
    lists = (
        pltpu.make_async_copy(counts, count, ssem.at[0]),
        pltpu.make_async_copy(ranks, rank, ssem.at[1]),
    )
    for copy in lists:
        copy.start()
    lax.fori_loop(0, blocks // span, fetch, 0)
    for copy in winds:
        copy.start()
    for copy in lists:
        copy.wait()
    lit = count[lax.axis_index("lat"), lax.axis_index("lon")]

    def mark(n, _):
        flag[rank[0, 0, n]] = jnp.where(n < lit, 0, 1)
        return 0

    lax.fori_loop(0, blocks, mark, 0, unroll=True)

    def sort(b, ends):
        first, final = ends
        dark = flag[b]
        order[jnp.where(dark == 0, first, final)] = b
        return first + 1 - dark, final + dark

    lax.fori_loop(0, blocks, sort, (0, lit), unroll=True)

    @pl.when(lit > 0)
    def _():
        start = arrive(0)
        for s in range(FIELDS):
            bring(s, start)

        def turn(n, _):
            @pl.when(n + 1 < lit)
            def _():
                arrive(n + 1)

            coming = order[jnp.minimum(n + 1, lit - 1)]
            leaving = jnp.where(n > 0, order[jnp.maximum(n - 1, 0)], blocks)
            def exchange(i):
                conclude(i, steps, tout, state, bufs)
                prepare(i, steps, tin, state, coef)

            first_stage(steps, state, bufs, coef, exchange)
            bring(FIELDS - 1, coming)
            later_stage(stage_consts(2), steps, bufs.at[1], state, bufs.at[0], state, coef)

            def pair(turn_pair, _):
                bring(turn_pair, coming)
                emit(jnp.minimum(turn_pair, species - 1), leaving)
                for q in range(2):
                    consts = [table[2 * turn_pair + q, c] for c in range(4)]
                    now, other = bufs.at[q], bufs.at[1 - q]
                    later_stage(consts, steps, now, other, other, state, coef)
                return 0

            lax.fori_loop(0, (SECTIONS - 2) // 2, pair, 0)
            return 0

        lax.fori_loop(0, lit, turn, 0)
        for i in range(steps):
            conclude(i, steps, tout, state, bufs)
        for s in range(species):
            emit(s, order[lit - 1])

    def night(n, _):
        b = arrive(n)
        ozone, oxygen, nitric, dioxide = (raw[s, b] for s in range(species))
        t = 0.5 * (ozone * nitric)
        values = (ozone + (0.75 * oxygen - t), oxygen - 0.75 * oxygen, nitric - t, dioxide + t)
        for s, value in enumerate(values):
            mix[s, place(b), :] = value
        return 0

    lax.fori_loop(lit, blocks, night, 0)
    for copy in winds:
        copy.wait()
    for s in range(species):
        lon_head[s] = mix[s, pl.ds(0, lat_cells), :]
        lon_tail[s] = mix[s, pl.ds((lon_cells - 1) * lat_cells, lat_cells), :]
        for i in range(lon_cells // SUB):
            start = i * SUB * lat_cells
            lat_head[s, rows(i), :] = mix[s, pl.ds(start, SUB, stride=lat_cells), :]
            lat_tail[s, rows(i), :] = mix[s, pl.ds(start + lat_cells - 1, SUB, stride=lat_cells), :]
    flat = wind.reshape(lon_cells * SUB, levels)
    for i in range(lon_cells // SUB):
        lat_tail[species, rows(i), :] = flat[pl.ds(i * SUB * SUB + SUB - 1, SUB, stride=SUB), :]


def buffer(*dims):
    return pltpu.VMEM(dims, jnp.float32)


ANYWHERE = pl.BlockSpec(memory_space=pl.ANY)
VECTORS = pl.BlockSpec(memory_space=pltpu.VMEM)


def in_hbm(x):
    return pltpu.with_memory_space_constraint(x, pltpu.HBM)


def in_vmem(x):
    return pltpu.with_memory_space_constraint(x, pltpu.VMEM)


def column_pass(count, order, tracers, kdiff, photolysis, u_wind, v_wind):
    species, lon_cells, lat_cells, levels = tracers.shape
    blocks = order.shape[2]
    cols = lon_cells * lat_cells // blocks
    return pl.pallas_call(
        column_kernel,
        in_specs=[ANYWHERE] * 7,
        out_specs=[VECTORS] * 5,
        out_shape=[
            buffer(species, (blocks + 1) * cols, levels),
            buffer(species + 1, lat_cells, levels),
            buffer(species, lat_cells, levels),
            buffer(species + 1, lon_cells, levels),
            buffer(species, lon_cells, levels),
        ],
        scratch_shapes=[
            buffer(FIELDS, blocks, cols, levels),
            buffer(FIELDS, levels + SUB, cols),
            buffer(species, levels + SUB, cols),
            buffer(species + 1, levels, cols),
            buffer(2, species, levels, cols),
            buffer(4, levels, cols),
            buffer(lon_cells, SUB, levels),
            pltpu.SMEM((SECTIONS - 2, 4), jnp.float32),
            pltpu.SMEM(count.shape, jnp.int32),
            pltpu.SMEM(order.shape, jnp.int32),
            pltpu.SMEM((blocks,), jnp.int32),
            pltpu.SMEM((blocks,), jnp.int32),
            pltpu.SMEM((blocks,), jnp.int32),
            pltpu.SemaphoreType.DMA((blocks // math.gcd(blocks, COPY),)),
            pltpu.SemaphoreType.DMA((2,)),
            pltpu.SemaphoreType.DMA((2,)),
        ],
        compiler_params=pltpu.CompilerParams(vmem_limit_bytes=24 << 20),
        name="columns",
    )(
        in_hbm(count),
        in_hbm(order),
        in_hbm(tracers.reshape(species, blocks, cols, levels)),
        in_hbm(kdiff.reshape(blocks, cols, levels)),
        in_hbm(photolysis.reshape(blocks, cols, levels)),
        in_hbm(u_wind),
        in_hbm(v_wind),
    )


def transport_kernel(
    mix, u, v, out, lon_rim, lat_rim, east_flux, stage, sem,
):
    lon_cells, lat_cells, levels = u.shape
    species = out.shape[0]
    tiles = lat_cells // SUB
    zero = jnp.zeros((SUB, levels), jnp.float32)
    row = lax.broadcasted_iota(jnp.int32, (SUB, levels), 0)
    for s in range(species):
        for t in range(tiles):
            east_flux[s, rows(t), :] = zero

    def line(i, last, put):
        base = pl.multiple_of(i * lat_cells, SUB)
        below = [zero] * species
        for t in range(tiles):
            wu, wv = u[i, rows(t), :], v[i, rows(t), :]
            east_going, north_going = wu > 0.0, wv > 0.0
            for s in range(species):
                here = mix[s, pl.ds(base + t * SUB, SUB), :]
                donor = 0.0 if last else mix[s, pl.ds(base + lat_cells + t * SUB, SUB), :]
                x_flux = wu * jnp.where(east_going, here, donor)
                if t < tiles - 1:
                    ahead = mix[s, pl.ds(base + t * SUB + 1, SUB), :]
                else:
                    ahead = jnp.where(row < SUB - 1, pltpu.roll(here, SUB - 1, axis=0), 0.0)
                y_flux = wv * jnp.where(north_going, here, ahead)
                turned = pltpu.roll(y_flux, 1, axis=0)
                y_loss = y_flux - jnp.where(row == 0, below[s], turned)
                below[s] = turned
                x_loss = x_flux - east_flux[s, rows(t), :]
                east_flux[s, rows(t), :] = x_flux
                put(s, t, (here - x_loss) - y_loss)

    def rim_row(side):
        def put(s, t, value):
            lon_rim[s, side, rows(t), :] = value

        return put

    def inner_row(i):
        def put(s, t, value):
            if 0 < t < tiles - 1:
                stage[s, i - 1, rows(t - 1), :] = value
            else:
                lat_rim[s, min(t, 1), i - 1] = value

        return put

    inner = pl.ds(SUB, lat_cells - 2 * SUB)

    def ship(i, count):
        return pltpu.make_async_copy(
            stage.at[:, pl.ds(i - 1, count)], out.at[:, pl.ds(i, count), inner], sem.at[0]
        )

    line(0, False, rim_row(0))

    def several(i, count):
        for q in range(count):
            line(i + q, False, inner_row(i + q))
        ship(i, count).start()

    def turn(n, _):
        several(1 + ROWS * n, ROWS)
        return 0

    turns, rest = (lon_cells - 2) // ROWS, (lon_cells - 2) % ROWS
    lax.fori_loop(0, turns, turn, 0)
    if rest:
        several(1 + ROWS * turns, rest)
    line(lon_cells - 1, True, rim_row(1))
    ship(1, lon_cells - 2).wait()


def transport(mix, u_wind, v_wind, species):
    lon_cells, lat_cells, levels = u_wind.shape
    return pl.pallas_call(
        transport_kernel,
        in_specs=[VECTORS] * 3,
        out_specs=[ANYWHERE] + [VECTORS] * 2,
        out_shape=[
            pltpu.HBM((species, lon_cells, lat_cells, levels), jnp.float32),
            buffer(species, 2, lat_cells, levels),
            buffer(species, 2, lon_cells - 2, SUB, levels),
        ],
        scratch_shapes=[
            buffer(species, lat_cells, levels),
            buffer(species, lon_cells - 2, lat_cells - 2 * SUB, levels),
            pltpu.SemaphoreType.DMA((1,)),
        ],
        compiler_params=pltpu.CompilerParams(vmem_limit_bytes=12 << 20),
        name="transport",
    )(in_vmem(mix), in_vmem(u_wind), in_vmem(v_wind))


def rim_kernel(
    partial, lon_rim, lat_rim, south, north, west, east, lon_tail, lon_head, lat_tail, lat_head,
    out, lon_new, lat_new, sem,
):
    species, lon_cells, lat_cells, levels = out.shape
    inner = lon_cells - 2
    wind = west[species]
    wind_out = jnp.minimum(lon_tail[species], 0.0)
    place = lax.axis_index("lat")
    south_wind = jnp.where(place > 0, south[species], 0.0)
    beyond = place < lax.axis_size("lat") - 1
    north_wind = jnp.where(beyond, jnp.minimum(lat_tail[species], 0.0), 0.0)
    copies = []
    for s in range(species):
        first = south_wind * jnp.where(south_wind > 0.0, south[s], lat_head[s])
        changes = (0, first), (lat_cells - 1, -(north_wind * north[s]))
        lon_new[s, 0] = lon_rim[s, 0] + wind * jnp.where(wind > 0.0, west[s], lon_head[s])
        lon_new[s, 1] = lon_rim[s, 1] - wind_out * east[s]
        for side, (at, change) in enumerate(changes):
            for q, i in ((0, 0), (1, lon_cells - 1)):
                lon_new[s, q, pl.ds(at, 1), :] = lon_new[s, q, pl.ds(at, 1), :] + change[i : i + 1, :]
            for i in range(inner):
                edge = (s, side, i, pl.ds(at % SUB, 1))
                rest = (s, side, i, pl.ds(1 - side, SUB - 1))
                lat_new[rest] = lat_rim[rest]
                lat_new[edge] = lat_rim[edge] + change[i + 1 : i + 2, :]
        for side, (i, start) in enumerate(((0, 0), (lon_cells - 1, lat_cells - SUB))):
            copies += [
                pltpu.make_async_copy(lon_new.at[s, side], out.at[s, i], sem.at[0, side, s]),
                pltpu.make_async_copy(
                    lat_new.at[s, side],
                    out.at[s, pl.ds(1, inner), pl.ds(start, SUB)],
                    sem.at[1, side, s],
                ),
            ]
        for copy in copies[-4:]:
            copy.start()
    for copy in copies:
        copy.wait()


def rim_pass(partial, rims, halos, edges):
    species, lon_cells, lat_cells, levels = partial.shape
    return pl.pallas_call(
        rim_kernel,
        in_specs=[ANYWHERE] + [VECTORS] * 10,
        out_specs=ANYWHERE,
        out_shape=pltpu.HBM(partial.shape, jnp.float32),
        input_output_aliases={0: 0},
        scratch_shapes=[
            buffer(species, 2, lat_cells, levels),
            buffer(species, 2, lon_cells - 2, SUB, levels),
            pltpu.SemaphoreType.DMA((2, 2, species)),
        ],
        compiler_params=pltpu.CompilerParams(vmem_limit_bytes=12 << 20),
        name="rim",
    )(in_hbm(partial), *(in_vmem(x) for x in (*rims, *halos, *edges)))


def body(tracers, kdiff, photolysis, u_wind, v_wind, day_count, day_order):
    mix, *edges = column_pass(
        day_count.T, day_order, tracers, kdiff, photolysis, u_wind, v_wind
    )
    lon_tail, lon_head, lat_tail, lat_head = edges

    def shift(edge, axis, step):
        size = lax.axis_size(axis)
        return lax.ppermute(edge, axis, [(i, (i + step) % size) for i in range(size)])

    south, north = shift(lat_tail, "lat", 1), shift(lat_head, "lat", -1)
    halos = (south, north, shift(lon_tail, "lon", 1), shift(lon_head, "lon", -1))
    partial, *rims = transport(mix, u_wind, v_wind, tracers.shape[0])
    return rim_pass(partial, rims, halos, edges)


def solution(mesh):
    return jax.shard_map(
        body,
        mesh=mesh,
        in_specs=(
            P(None, "lon", "lat", None),
            P("lon", "lat", None),
            P("lon", "lat", None),
            P("lon", "lat", None),
            P("lon", "lat", None),
            P(),
            P("lon", "lat", None),
        ),
        out_specs=P(None, "lon", "lat", None),
        check_vma=False,
    )
```
